32 devices in a mesh: groups: 2 (over x), dp: 2 (over core), tensor: 8 (over z, y).
Axes of the slice: x: 2, y: 2, z: 4, core: 2. Of those that a mesh axis runs over, the one named last changes fastest.
Arguments:
- convolution_branch_input: bfloat16 [256, 3, 16384], P(('groups', 'dp'), None, 'tensor'), parts along dimension 0, may hold values from -6 to 6
- gate_branch_input: bfloat16 [256, 3, 16384], P(('groups', 'dp'), None, 'tensor'), parts along dimension 0, may hold values from -6 to 6
- convolution_state: bfloat16 [256, 3, 16384], P(('groups', 'dp'), None, 'tensor'), parts along dimension 0, may hold values from -6 to 6
- initial_hidden_state: float32 [256, 16, 16384], P(('groups', 'dp'), None, 'tensor'), parts along dimension 0, may hold values from -6 to 6
- stream_adapter_index: int32 [256], P(('groups', 'dp')), parts along dimension 0, may hold values from 0 to 31, as said below
- convolution_weight: float32 [4, 16384], P(None, 'tensor'), may hold values from -3 to 3
- convolution_bias: float32 [16384], P('tensor'), may hold values from -3 to 3
- input_coefficient_projection: bfloat16 [16384, 544], P('tensor'), may hold values from -0.046875 to 0.046875
- step_size_norm_gain: float32 [512], replicated, may hold values from 0.1 to 1.9
- step_size_projection: bfloat16 [512, 16384], P(None, 'tensor'), may hold values from -0.25 to 0.25
- step_size_bias: float32 [16384], P('tensor'), may hold values from -4 to -1
- negated_diagonal: float32 [16, 16384], P(None, 'tensor'), may hold values from 0.5 to 16
- channel_skip_gain: float32 [16384], P('tensor'), may hold values from 0.5 to 1.5
- output_projection: bfloat16 [16384, 8192], P('tensor'), may hold values from -0.0625 to 0.0625
- adapter_down_factor: bfloat16 [32, 16384, 64], P(('dp', 'tensor')), may hold values from -0.046875 to 0.046875
- adapter_up_factor: bfloat16 [32, 64, 8192], P(('dp', 'tensor')), may hold values from -0.75 to 0.75
Outputs:
- layer_out: bfloat16 [256, 3, 8192], P(('groups', 'dp'), None, 'tensor'), parts along dimension 0
- state_out: float32 [256, 16, 16384], P(('groups', 'dp'), None, 'tensor'), parts along dimension 0
The draws below stay inside these ranges and needn't reach their ends.
There are 2 independent parts, one for each index of `groups`. The reference program is written for one: setup_inputs(seed, part) draws one part's arguments, and reference() takes and returns one part's arrays. A program takes and returns all parts, laid end to end along the dimension named above; an argument that names none is the same for every part. Nothing has to cross between parts.
Inputs may be any that keep to these rules, and one draw needn't show every extreme that they name: `stream_adapter_index`: adapter a is held by the device of index a // 2 over dp and tensor together (dp slowest). Among the streams of one dp shard at most 8 use adapters of one owner device, and in every shard some owner device has exactly 8 of them.
All inputs are finite; a program needn't handle non-finite values.
Results may differ from the reference program's by a relative error of at most 0.0063.
Values may be sent and summed in bfloat16 or wider, within the bound.
A program may use at most 192 MiB of HBM per device.

```python
import math
import jax
import jax.numpy as jnp
from jax import lax

MODEL_WIDTH = 8192
INNER_CHANNELS = 16384
N = 16
KCONV = 4
DT_RANK = 512
ADAPTER_RANK = 64
STEPS = 3
ADP_DEV = 2
S_DEV = 64
STREAMS = 128
OWNER_DEVICES = 16
ADAPTER_TOTAL = 32
CAP = 8
N_DP = 2


def pick_shard(key):
    perm_key, score_random_key, local_key, order_key = jax.random.split(key, 4)
    adapter_bank = OWNER_DEVICES * CAP
    table_entry = jnp.arange(adapter_bank, dtype=jnp.int32)
    owner_of = table_entry // CAP
    ranking = jax.random.permutation(perm_key, OWNER_DEVICES).astype(jnp.int32)
    current_tally = ranking[owner_of]
    larger_value = 1 << 20
    extra_credit = jnp.where(current_tally == 0, 2 * larger_value, jnp.where(current_tally < max(1, OWNER_DEVICES // 8), larger_value, 0))
    owner_score = (extra_credit + jax.random.randint(score_random_key, (adapter_bank,), 0, larger_value, dtype=jnp.int32)) * adapter_bank + table_entry
    chosen = jnp.argsort(-owner_score)[:S_DEV]
    chosen_owner = owner_of[chosen]
    local = jax.random.randint(local_key, (S_DEV,), 0, ADP_DEV, dtype=jnp.int32)
    idents = chosen_owner * ADP_DEV + local
    shuffle = jax.random.permutation(order_key, S_DEV)
    return idents[shuffle].astype(jnp.int32)


def draw_stream_adapter_index(key, part):
    key = jax.random.fold_in(key, 11)
    shard_keys = jax.random.split(key, N_DP)
    return jax.vmap(pick_shard)(shard_keys).reshape(-1).astype(jnp.int32)


def spiked(values, stream_key, source, target, shards_of, factor):
    owner, partner = [(jnp.arange(values.shape[axis_at]) // (values.shape[axis_at] // shards_of)).reshape([-1 if axis == axis_at else 1 for axis in range(values.ndim)]) for axis_at in (source, target)]
    chosen = jax.random.permutation(stream_key, shards_of)[partner]
    strong = (owner == chosen) | (owner == (partner + shards_of // 2) % shards_of)
    return jnp.where(strong, factor * values, values)


def steps_of(rng, dims, cuts, smallest, largest):
    loudness, own = 1.0, jax.random.fold_in(rng, 6)
    for axis_at, blocks in cuts:
        steps = jnp.exp(jax.random.uniform(jax.random.fold_in(own, axis_at), (blocks,), jnp.float32, smallest / len(cuts), largest / len(cuts)))
        loudness = loudness * jnp.repeat(steps, dims[axis_at] // blocks).reshape([-1 if axis == axis_at else 1 for axis in range(len(dims))])
    return loudness


def normal_values(own_key, extent, deviation, bound, cuts=(), held_as=jnp.bfloat16):
    array = deviation * jax.random.normal(own_key, extent, jnp.float32)
    if cuts:
        array = array * steps_of(own_key, extent, cuts, -0.22, 0.18)
    return jnp.clip(array, -bound, bound).astype(held_as)


def gaussian_with(key, dims, width, limit, pieces, heavy, held_as=jnp.bfloat16):
    entries = width * jax.random.normal(key, dims, jnp.float32)
    if pieces:
        entries = entries * steps_of(key, dims, pieces, -0.22, 0.18)
    return jnp.clip(spiked(entries, jax.random.fold_in(key, 3), *heavy), -limit, limit).astype(held_as)


def setup_inputs(seed: int = 0, part: int = 0) -> dict:
    streams_of = jax.random.split(jax.random.key(seed), 17)
    own_keys = jax.random.split(jax.random.fold_in(streams_of[16], part), 17)
    return {
        "convolution_branch_input": normal_values(own_keys[0], (STREAMS, STEPS, INNER_CHANNELS), 1.0, 6.0, ((0, 2), (2, 8))),
        "gate_branch_input": normal_values(own_keys[1], (STREAMS, STEPS, INNER_CHANNELS), 1.0, 6.0, ((0, 2), (2, 8))),
        "convolution_state": normal_values(own_keys[2], (STREAMS, KCONV - 1, INNER_CHANNELS), 1.0, 6.0, ((0, 2), (2, 8))),
        "initial_hidden_state": normal_values(own_keys[3], (STREAMS, N, INNER_CHANNELS), 1.0, 6.0, ((0, 2), (2, 8)), jnp.float32),
        "stream_adapter_index": draw_stream_adapter_index(jax.random.fold_in(jax.random.fold_in(streams_of[16], part), 71), part),
        "convolution_weight": normal_values(streams_of[5], (KCONV, INNER_CHANNELS), KCONV ** -0.5, 3.0, ((1, 8),), jnp.float32),
        "convolution_bias": normal_values(streams_of[6], (INNER_CHANNELS,), 0.5, 3.0, ((0, 8),), jnp.float32),
        "input_coefficient_projection": normal_values(streams_of[7], (INNER_CHANNELS, DT_RANK + 2 * N), INNER_CHANNELS ** -0.5, 0.046875, ((0, 8),)),
        "step_size_norm_gain": jnp.clip(1.0 + 0.18 * jax.random.normal(streams_of[8], (DT_RANK,), jnp.float32), 0.1, 1.9),
        "step_size_projection": normal_values(streams_of[9], (DT_RANK, INNER_CHANNELS), DT_RANK ** -0.5, 0.25, ((1, 8),)),
        "step_size_bias": jnp.clip(-4.0 + 3.0 * jax.random.uniform(streams_of[10], (INNER_CHANNELS,), jnp.float32) ** steps_of(streams_of[10], (INNER_CHANNELS,), ((0, 8),), -0.2, 0.2), -4.0, -1.0),
        "negated_diagonal": jnp.clip(jnp.exp(math.log(16.0) - 3.465736 * jax.random.uniform(streams_of[11], (N, INNER_CHANNELS), jnp.float32) ** steps_of(streams_of[11], (N, INNER_CHANNELS), ((1, 8),), -0.2, 0.2)), 0.5, 16.0),
        "channel_skip_gain": jnp.clip(0.5 + 1.0 * jax.random.uniform(streams_of[12], (INNER_CHANNELS,), jnp.float32) ** steps_of(streams_of[12], (INNER_CHANNELS,), ((0, 8),), -0.2, 0.2), 0.5, 1.5),
        "output_projection": gaussian_with(streams_of[13], (INNER_CHANNELS, MODEL_WIDTH), INNER_CHANNELS ** -0.5, 0.0625, ((0, 8),), (0, 1, 8, 2.0)),
        "adapter_down_factor": normal_values(streams_of[14], (ADAPTER_TOTAL, INNER_CHANNELS, ADAPTER_RANK), INNER_CHANNELS ** -0.5, 0.046875, ((0, 16),)),
        "adapter_up_factor": normal_values(streams_of[15], (ADAPTER_TOTAL, ADAPTER_RANK, MODEL_WIDTH), ADAPTER_RANK ** -0.5, 0.75, ((0, 16),)),
    }


def reference(convolution_branch_input, gate_branch_input, convolution_state, initial_hidden_state, stream_adapter_index, convolution_weight, convolution_bias, input_coefficient_projection, step_size_norm_gain, step_size_projection, step_size_bias, negated_diagonal, channel_skip_gain, output_projection, adapter_down_factor, adapter_up_factor):
    full = jnp.concatenate([convolution_state, convolution_branch_input], axis=1)
    state = initial_hidden_state
    gathered = []
    for step in range(STEPS):
        window = full[:, step:step + KCONV].astype(jnp.float32)
        mixed = lax.optimization_barrier(jnp.sum(window * convolution_weight[None], axis=1)) + convolution_bias
        conv_out = jax.nn.silu(mixed)
        conv_low = conv_out.astype(jnp.bfloat16)
        projected = jnp.dot(conv_low, input_coefficient_projection, preferred_element_type=jnp.float32)
        dt_raw = projected[:, :DT_RANK]
        in_coef = projected[:, DT_RANK:DT_RANK + N]
        out_coef = projected[:, DT_RANK + N:]
        factor = lax.rsqrt(lax.optimization_barrier(jnp.mean(dt_raw * dt_raw, axis=1, keepdims=True)) + 1e-06)
        dt_low = (dt_raw * factor * step_size_norm_gain).astype(jnp.bfloat16)
        step_size = jax.nn.softplus(jnp.dot(dt_low, step_size_projection, preferred_element_type=jnp.float32) + step_size_bias)
        decay = jnp.exp(-step_size[:, None, :] * negated_diagonal[None])
        state = decay * state + step_size[:, None, :] * in_coef[:, :, None] * conv_out[:, None, :]
        read = lax.optimization_barrier(jnp.sum(state * out_coef[:, :, None], axis=1)) + channel_skip_gain * conv_out
        gated = read * jax.nn.silu(gate_branch_input[:, step].astype(jnp.float32))
        gathered.append(gated.astype(jnp.bfloat16))
    inner_y = jnp.stack(gathered, axis=1)
    streams = inner_y.shape[0]
    base = jnp.dot(inner_y.reshape(streams * STEPS, INNER_CHANNELS), output_projection, preferred_element_type=jnp.float32)
    base = base.reshape(streams, STEPS, MODEL_WIDTH)

    def adapt(pair):
        rows, identity_label = pair
        down_factor = lax.dynamic_index_in_dim(adapter_down_factor, identity_label.astype(jnp.int32), 0, keepdims=False)
        up_factor = lax.dynamic_index_in_dim(adapter_up_factor, identity_label.astype(jnp.int32), 0, keepdims=False)
        coeffs = jnp.dot(rows, down_factor, preferred_element_type=jnp.float32).astype(jnp.bfloat16)
        return jnp.dot(coeffs, up_factor, preferred_element_type=jnp.float32).astype(jnp.bfloat16)
    delta = lax.map(adapt, (inner_y, stream_adapter_index))
    layer_out = (base + delta.astype(jnp.float32)).astype(jnp.bfloat16)
    return (layer_out, state)
```

```python
import functools

import jax
import jax.numpy as jnp
from jax import lax
from jax.experimental import pallas as pl
from jax.experimental.pallas import tpu as pltpu
from jax.sharding import PartitionSpec as P

MESH = pl.DeviceIdType.MESH


def norm_kernel(parts, dt_rank, part_ref, gain_ref, dt_ref, coef_ref, held, send_sem, recv_sem, send2, recv2, send3, recv3):
    me = lax.axis_index("tensor")
    barrier = pltpu.get_barrier_semaphore()
    for k in range(1, parts):
        peer = lax.rem(me + k, parts)
        pl.semaphore_signal(barrier, inc=1, device_id={"tensor": peer}, device_id_type=MESH)
    pl.semaphore_wait(barrier, parts - 1)
    copies = []
    for k in range(1, parts):
        peer = lax.rem(me + k, parts)
        copy = pltpu.make_async_remote_copy(
            src_ref=part_ref.at[peer],
            dst_ref=held.at[k - 1],
            send_sem=send_sem.at[k - 1],
            recv_sem=recv_sem.at[k - 1],
            device_id={"tensor": peer},
            device_id_type=MESH,
        )
        copy.start()
        copies.append(copy)
    total = part_ref[me]
    for k in range(1, parts):
        copies[k - 1].wait_recv()
        total = total + held[k - 1]
    dt_raw = total[:, :dt_rank]
    factor = lax.rsqrt(jnp.mean(dt_raw * dt_raw, axis=1, keepdims=True) + 1e-06)
    dt_low = dt_raw * factor * gain_ref[...]
    rows = dt_low.shape[0]
    padded = dt_ref.shape[1]
    if padded > rows:
        dt_low = jnp.concatenate([dt_low, jnp.zeros((padded - rows, dt_rank), jnp.float32)], axis=0)
    dt_ref[me] = dt_low.astype(jnp.bfloat16)
    coef_ref[me] = total[:, dt_rank:]
    later = []
    for k in range(1, parts):
        peer = lax.rem(me + k, parts)
        for ref, out_sem, in_sem in ((dt_ref, send2, recv2), (coef_ref, send3, recv3)):
            copy = pltpu.make_async_remote_copy(
                src_ref=ref.at[me],
                dst_ref=ref.at[me],
                send_sem=out_sem.at[k - 1],
                recv_sem=in_sem.at[k - 1],
                device_id={"tensor": peer},
                device_id_type=MESH,
            )
            copy.start()
            later.append(copy)
    for copy in copies:
        copy.wait_send()
    for copy in later:
        copy.wait()


def summed_and_normed(partial, gain, parts, dt_rank):
    rows, columns = partial.shape
    share = rows // parts
    padded = -(-share // 16) * 16
    dma = pltpu.SemaphoreType.DMA((parts - 1,))
    dt, coef = pl.pallas_call(
        functools.partial(norm_kernel, parts, dt_rank),
        out_shape=(
            jax.ShapeDtypeStruct((parts, padded, dt_rank), jnp.bfloat16),
            jax.ShapeDtypeStruct((parts, share, columns - dt_rank), jnp.float32),
        ),
        in_specs=[pl.BlockSpec(memory_space=pltpu.VMEM)] * 2,
        out_specs=(pl.BlockSpec(memory_space=pltpu.VMEM),) * 2,
        scratch_shapes=[
            pltpu.VMEM((parts - 1, share, columns), jnp.float32),
        ]
        + [dma] * 6,
        compiler_params=pltpu.CompilerParams(
            collective_id=0, has_side_effects=True, vmem_limit_bytes=24 << 20
        ),
    )(partial.reshape(parts, share, columns), gain.reshape(1, dt_rank))
    return dt[:, :share].reshape(rows, dt_rank), coef.reshape(rows, columns - dt_rank)


def scatter_kernel(x_ref, out_ref, r0, r1, r2, a1, a2, send_sem, recv_sem):
    me = lax.axis_index("tensor")
    y, z = lax.rem(me, 2), me // 2
    h = z // 2
    c = lax.rem(z + h, 2)
    bits = (y, c, h)

    def place(sel):
        far = sel[1] + sel[2] * (3 - 2 * sel[1])
        return far * 2 + sel[0]

    def flipped(d):
        return tuple(1 - b if i == d else b for i, b in enumerate(bits))

    barrier = pltpu.get_barrier_semaphore()
    for d in range(3):
        pl.semaphore_signal(barrier, inc=1, device_id={"tensor": place(flipped(d))}, device_id_type=MESH)
    pl.semaphore_wait(barrier, 3)
    width = out_ref.shape[1]
    half = width // 2
    orders = ((0, 1, 2), (1, 2, 0))

    def send(flow, n, src, dst, d):
        copy = pltpu.make_async_remote_copy(
            src_ref=src,
            dst_ref=dst,
            send_sem=send_sem.at[flow * 7 + n],
            recv_sem=recv_sem.at[flow * 7 + n],
            device_id={"tensor": place(flipped(d))},
            device_id_type=MESH,
        )
        copy.start()
        return copy

    def columns(flow, sel):
        return pl.ds(pl.multiple_of(place(sel) * width + flow * half, 128), half)

    def chosen(order, values):
        sel = [None] * 3
        for d, v in zip(order, values):
            sel[d] = v
        return tuple(sel)

    first, second, third = [[], []], [[], []], [None, None]
    for p in range(2):
        for q in range(2):
            for flow in range(2):
                o = orders[flow]
                b1 = 1 - bits[o[1]] if p == 0 else bits[o[1]]
                sel = chosen(o, (1 - bits[o[0]], b1, q))
                first[flow].append(send(flow, p * 2 + q, x_ref.at[:, columns(flow, sel)], r0.at[flow, p * 2 + q], o[0]))
    for q in range(2):
        for flow in range(2):
            o = orders[flow]
            first[flow][q].wait_recv()
            sel = chosen(o, (bits[o[0]], 1 - bits[o[1]], q))
            own = x_ref[:, columns(flow, sel)].astype(jnp.float32)
            a1[flow, q] = (own + r0[flow, q].astype(jnp.float32)).astype(jnp.bfloat16)
            second[flow].append(send(flow, 4 + q, a1.at[flow, q], r1.at[flow, q], o[1]))
    for q in range(2):
        for flow in range(2):
            o = orders[flow]
            first[flow][2 + q].wait_recv()
            sel = chosen(o, (bits[o[0]], bits[o[1]], q))
            own = x_ref[:, columns(flow, sel)].astype(jnp.float32)
            a2[flow, q] = own + r0[flow, 2 + q].astype(jnp.float32)
    for flow in range(2):
        o = orders[flow]
        for q in range(2):
            second[flow][q].wait_recv()
        want = 1 - bits[o[2]]
        a1[flow, 2] = (a2[flow, want] + r1[flow, want].astype(jnp.float32)).astype(jnp.bfloat16)
        third[flow] = send(flow, 6, a1.at[flow, 2], r2.at[flow], o[2])
    for flow in range(2):
        o = orders[flow]
        keep = bits[o[2]]
        third[flow].wait_recv()
        out_ref[:, flow * half : (flow + 1) * half] = (
            a2[flow, keep] + r1[flow, keep].astype(jnp.float32) + r2[flow].astype(jnp.float32)
        ).astype(jnp.bfloat16)
    for flow in range(2):
        for copy in first[flow] + second[flow] + [third[flow]]:
            copy.wait_send()


def scattered(partial, parts):
    rows, width = partial.shape
    own = width // parts
    half = own // 2
    return pl.pallas_call(
        scatter_kernel,
        out_shape=jax.ShapeDtypeStruct((rows, own), jnp.bfloat16),
        in_specs=[pl.BlockSpec(memory_space=pltpu.VMEM)],
        out_specs=pl.BlockSpec(memory_space=pltpu.VMEM),
        scratch_shapes=[
            pltpu.VMEM((2, 4, rows, half), jnp.bfloat16),
            pltpu.VMEM((2, 2, rows, half), jnp.bfloat16),
            pltpu.VMEM((2, rows, half), jnp.bfloat16),
            pltpu.VMEM((2, 3, rows, half), jnp.bfloat16),
            pltpu.VMEM((2, 2, rows, half), jnp.float32),
            pltpu.SemaphoreType.DMA((14,)),
            pltpu.SemaphoreType.DMA((14,)),
        ],
        compiler_params=pltpu.CompilerParams(
            collective_id=1, has_side_effects=True, vmem_limit_bytes=32 << 20
        ),
    )(partial)


def body(
    convolution_branch_input,
    gate_branch_input,
    convolution_state,
    initial_hidden_state,
    stream_adapter_index,
    convolution_weight,
    convolution_bias,
    input_coefficient_projection,
    step_size_norm_gain,
    step_size_projection,
    step_size_bias,
    negated_diagonal,
    channel_skip_gain,
    output_projection,
    adapter_down_factor,
    adapter_up_factor,
):
    n_dp = lax.axis_size("dp")
    tensor_parts = lax.axis_size("tensor")
    owners = n_dp * tensor_parts
    streams, steps, channel_count = convolution_branch_input.shape
    dt_rank = step_size_norm_gain.shape[0]
    states = negated_diagonal.shape[0]
    kernel = convolution_weight.shape[0]
    width = output_projection.shape[1]
    slice_part = width // tensor_parts
    owner_share = adapter_down_factor.shape[0]
    rank_width = adapter_down_factor.shape[2]
    capacity = max(2, 2 * streams // owners)
    full = jnp.concatenate([convolution_state, convolution_branch_input], axis=1)
    state = initial_hidden_state
    gathered = []
    conv_outs = []
    for step in range(steps):
        window = full[:, step : step + kernel].astype(jnp.float32)
        mixed = jnp.sum(window * convolution_weight[None], axis=1) + convolution_bias
        conv_outs.append(jax.nn.silu(mixed))
    conv_low = jnp.concatenate(conv_outs, axis=0).astype(jnp.bfloat16)
    partial_proj = jnp.dot(
        conv_low, input_coefficient_projection, preferred_element_type=jnp.float32
    )
    small = tensor_parts == 8 and n_dp == 2
    if small:
        dt_all, coef_all = summed_and_normed(
            partial_proj, step_size_norm_gain, tensor_parts, dt_rank
        )
    else:
        projected = lax.psum(partial_proj, "tensor")
        dt_raw = projected[:, :dt_rank]
        factor = lax.rsqrt(jnp.mean(dt_raw * dt_raw, axis=1, keepdims=True) + 1e-06)
        dt_all = (dt_raw * factor * step_size_norm_gain).astype(jnp.bfloat16)
        coef_all = projected[:, dt_rank:]
    for step in range(steps):
        conv_out = conv_outs[step]
        dt_low = dt_all[step * streams : (step + 1) * streams]
        coef = coef_all[step * streams : (step + 1) * streams]
        in_coef = coef[:, :states]
        out_coef = coef[:, states:]
        step_size = jax.nn.softplus(
            jnp.dot(dt_low, step_size_projection, preferred_element_type=jnp.float32)
            + step_size_bias
        )
        decay = jnp.exp(-step_size[:, None, :] * negated_diagonal[None])
        state = decay * state + step_size[:, None, :] * in_coef[:, :, None] * conv_out[:, None, :]
        read = jnp.sum(state * out_coef[:, :, None], axis=1) + channel_skip_gain * conv_out
        gated = read * jax.nn.silu(gate_branch_input[:, step].astype(jnp.float32))
        gathered.append(gated.astype(jnp.bfloat16))
    inner_y = jnp.stack(gathered, axis=1)
    owner = stream_adapter_index // owner_share
    local = stream_adapter_index % owner_share
    position = jnp.arange(streams, dtype=jnp.int32)
    before = (owner[:, None] == owner[None, :]) & (position[None, :] < position[:, None])
    current_tally = jnp.sum(before.astype(jnp.int32), axis=1)
    slot = owner * capacity + current_tally
    match = jnp.arange(owners * capacity, dtype=jnp.int32)[:, None] == slot[None, :]
    dispatch = match.astype(jnp.bfloat16)
    slot_local = jnp.sum(jnp.where(match, local[None, :], 0), axis=1).reshape(owners, capacity)
    outgoing = jnp.dot(
        dispatch,
        inner_y.reshape(streams, steps * channel_count),
        preferred_element_type=jnp.float32,
    )
    outgoing = outgoing.astype(jnp.bfloat16).reshape(owners, capacity, steps, channel_count)
    down_factor = adapter_down_factor.reshape(owner_share, tensor_parts, channel_count, rank_width)
    rows = lax.all_to_all(outgoing, ("dp", "tensor"), split_axis=0, concat_axis=0, tiled=True)
    idents = lax.all_to_all(slot_local, ("dp", "tensor"), split_axis=0, concat_axis=0, tiled=True)
    count = rows.shape[1]
    rows = rows.reshape(n_dp, tensor_parts, count, steps, channel_count)
    which = idents.reshape(n_dp, tensor_parts, count)[:, 0]
    select = (which[..., None] == jnp.arange(owner_share, dtype=jnp.int32)).astype(jnp.float32)
    every = jnp.einsum("itksc,atcr->iksar", rows, down_factor, preferred_element_type=jnp.float32)
    coeffs = jnp.einsum("iksar,ika->iksr", every, select).astype(jnp.bfloat16)
    if small:
        spread = jnp.einsum(
            "iksr,arc->iksac", coeffs, adapter_up_factor, preferred_element_type=jnp.float32
        )
        delta = jnp.einsum("iksac,ika->iksc", spread, select).astype(jnp.bfloat16)
        back = lax.all_to_all(delta, "dp", split_axis=0, concat_axis=0, tiled=True)
        mine = lax.axis_index("tensor")
        near = lax.dynamic_index_in_dim(
            dispatch.reshape(n_dp, tensor_parts, capacity, streams), mine, 1, keepdims=False
        )
        carried = jnp.dot(
            near.reshape(n_dp * capacity, streams).T,
            back.reshape(n_dp * capacity, steps * width),
            preferred_element_type=jnp.float32,
        )
        flat_rows = inner_y.reshape(streams * steps, channel_count)
        partial_value = jnp.dot(flat_rows, output_projection, preferred_element_type=jnp.float32)
        partial_value = partial_value + carried.reshape(streams * steps, width)
        total = scattered(partial_value.astype(jnp.bfloat16), tensor_parts)
        layer_out = total.reshape(streams, steps, slice_part)
    else:
        up_factor_split = adapter_up_factor.reshape(owner_share, rank_width, tensor_parts, slice_part)
        spread = jnp.einsum(
            "iksr,arjc->ijksac", coeffs, up_factor_split, preferred_element_type=jnp.float32
        )
        delta = jnp.einsum("ijksac,ika->ijksc", spread, select).astype(jnp.bfloat16)
        delta = delta.reshape(owners, count, steps, slice_part)
        back = lax.all_to_all(delta, ("dp", "tensor"), split_axis=0, concat_axis=0, tiled=True)
        flat_rows = inner_y.reshape(streams * steps, channel_count)
        partial_value = jnp.dot(flat_rows, output_projection, preferred_element_type=jnp.float32)
        total = lax.psum_scatter(
            partial_value.reshape(streams, steps, width), "tensor", scatter_dimension=2, tiled=True
        )
        carried = jnp.dot(
            dispatch.T,
            back.reshape(owners * capacity, steps * slice_part),
            preferred_element_type=jnp.float32,
        )
        layer_out = (total + carried.reshape(streams, steps, slice_part)).astype(jnp.bfloat16)
    return (layer_out, state)


def solution(mesh):
    placed = (
        P(("groups", "dp"), None, "tensor"),
        P(("groups", "dp"), None, "tensor"),
        P(("groups", "dp"), None, "tensor"),
        P(("groups", "dp"), None, "tensor"),
        P(("groups", "dp")),
        P(None, "tensor"),
        P("tensor"),
        P("tensor", None),
        P(),
        P(None, "tensor"),
        P("tensor"),
        P(None, "tensor"),
        P("tensor"),
        P("tensor", None),
        P(("dp", "tensor"), None, None),
        P(("dp", "tensor"), None, None),
    )
    return jax.shard_map(
        body,
        mesh=mesh,
        in_specs=placed,
        out_specs=(P(("groups", "dp"), None, "tensor"), P(("groups", "dp"), None, "tensor")),
        check_vma=False,
    )
```

```python
import functools

import jax
import jax.numpy as jnp
from jax import lax
from jax.experimental import pallas as pl
from jax.experimental.pallas import tpu as pltpu
from jax.sharding import PartitionSpec as P

MESH = pl.DeviceIdType.MESH


def norm_kernel(parts, dt_rank, part_ref, gain_ref, dt_ref, coef_ref, held, send_sem, recv_sem, send2, recv2, send3, recv3):
    me = lax.axis_index("tensor")
    barrier = pltpu.get_barrier_semaphore()
    for k in range(1, parts):
        peer = lax.rem(me + k, parts)
        pl.semaphore_signal(barrier, inc=1, device_id={"tensor": peer}, device_id_type=MESH)
    pl.semaphore_wait(barrier, parts - 1)
    copies = []
    for k in range(1, parts):
        peer = lax.rem(me + k, parts)
        copy = pltpu.make_async_remote_copy(
            src_ref=part_ref.at[peer],
            dst_ref=held.at[k - 1],
            send_sem=send_sem.at[k - 1],
            recv_sem=recv_sem.at[k - 1],
            device_id={"tensor": peer},
            device_id_type=MESH,
        )
        copy.start()
        copies.append(copy)
    total = part_ref[me]
    for k in range(1, parts):
        copies[k - 1].wait_recv()
        total = total + held[k - 1]
    dt_raw = total[:, :dt_rank]
    factor = lax.rsqrt(jnp.mean(dt_raw * dt_raw, axis=1, keepdims=True) + 1e-06)
    dt_low = dt_raw * factor * gain_ref[...]
    rows = dt_low.shape[0]
    padded = dt_ref.shape[1]
    if padded > rows:
        dt_low = jnp.concatenate([dt_low, jnp.zeros((padded - rows, dt_rank), jnp.float32)], axis=0)
    dt_ref[me] = dt_low.astype(jnp.bfloat16)
    coef_ref[me] = total[:, dt_rank:]
    later = []
    for k in range(1, parts):
        peer = lax.rem(me + k, parts)
        for ref, out_sem, in_sem in ((dt_ref, send2, recv2), (coef_ref, send3, recv3)):
            copy = pltpu.make_async_remote_copy(
                src_ref=ref.at[me],
                dst_ref=ref.at[me],
                send_sem=out_sem.at[k - 1],
                recv_sem=in_sem.at[k - 1],
                device_id={"tensor": peer},
                device_id_type=MESH,
            )
            copy.start()
            later.append(copy)
    for copy in copies:
        copy.wait_send()
    for copy in later:
        copy.wait()


def summed_and_normed(partial, gain, parts, dt_rank):
    rows, columns = partial.shape
    share = rows // parts
    padded = -(-share // 16) * 16
    dma = pltpu.SemaphoreType.DMA((parts - 1,))
    dt, coef = pl.pallas_call(
        functools.partial(norm_kernel, parts, dt_rank),
        out_shape=(
            jax.ShapeDtypeStruct((parts, padded, dt_rank), jnp.bfloat16),
            jax.ShapeDtypeStruct((parts, share, columns - dt_rank), jnp.float32),
        ),
        in_specs=[pl.BlockSpec(memory_space=pltpu.VMEM)] * 2,
        out_specs=(pl.BlockSpec(memory_space=pltpu.VMEM),) * 2,
        scratch_shapes=[
            pltpu.VMEM((parts - 1, share, columns), jnp.float32),
        ]
        + [dma] * 6,
        compiler_params=pltpu.CompilerParams(
            collective_id=0, has_side_effects=True, vmem_limit_bytes=24 << 20
        ),
    )(partial.reshape(parts, share, columns), gain.reshape(1, dt_rank))
    return dt[:, :share].reshape(rows, dt_rank), coef.reshape(rows, columns - dt_rank)


def scatter_kernel(base_ref, spot_ref, back_ref, out_ref, x_ref, r0, r1, r2, a1, a2, send_sem, recv_sem):
    me = lax.axis_index("tensor")
    y, z = lax.rem(me, 2), me // 2
    h = z // 2
    c = lax.rem(z + h, 2)
    bits = (y, c, h)

    def place(sel):
        far = sel[1] + sel[2] * (3 - 2 * sel[1])
        return far * 2 + sel[0]

    def flipped(d):
        return tuple(1 - b if i == d else b for i, b in enumerate(bits))

    barrier = pltpu.get_barrier_semaphore()
    for d in range(3):
        pl.semaphore_signal(barrier, inc=1, device_id={"tensor": place(flipped(d))}, device_id_type=MESH)
    pl.semaphore_wait(barrier, 3)
    width = out_ref.shape[1]
    half = width // 2
    orders = ((0, 1, 2), (1, 2, 0))

    def send(flow, n, src, dst, d):
        copy = pltpu.make_async_remote_copy(
            src_ref=src,
            dst_ref=dst,
            send_sem=send_sem.at[flow * 7 + n],
            recv_sem=recv_sem.at[flow * 7 + n],
            device_id={"tensor": place(flipped(d))},
            device_id_type=MESH,
        )
        copy.start()
        return copy

    def columns(flow, sel):
        return pl.ds(pl.multiple_of(place(sel) * width + flow * half, 128), half)

    def block(flow, sel):
        where = columns(flow, sel)
        extra = jnp.dot(spot_ref[...], back_ref[:, where], preferred_element_type=jnp.float32)
        return base_ref[:, where] + extra

    def chosen(order, values):
        sel = [None] * 3
        for d, v in zip(order, values):
            sel[d] = v
        return tuple(sel)

    first, second, third = [[], []], [[], []], [None, None]
    for p in range(2):
        for q in range(2):
            for flow in range(2):
                o = orders[flow]
                b1 = 1 - bits[o[1]] if p == 0 else bits[o[1]]
                sel = chosen(o, (1 - bits[o[0]], b1, q))
                n = p * 2 + q
                x_ref[flow, n] = block(flow, sel).astype(jnp.bfloat16)
                first[flow].append(send(flow, n, x_ref.at[flow, n], r0.at[flow, n], o[0]))
    for q in range(2):
        for flow in range(2):
            o = orders[flow]
            first[flow][q].wait_recv()
            sel = chosen(o, (bits[o[0]], 1 - bits[o[1]], q))
            own = block(flow, sel)
            a1[flow, q] = (own + r0[flow, q].astype(jnp.float32)).astype(jnp.bfloat16)
            second[flow].append(send(flow, 4 + q, a1.at[flow, q], r1.at[flow, q], o[1]))
    for q in range(2):
        for flow in range(2):
            o = orders[flow]
            first[flow][2 + q].wait_recv()
            sel = chosen(o, (bits[o[0]], bits[o[1]], q))
            own = block(flow, sel)
            a2[flow, q] = own + r0[flow, 2 + q].astype(jnp.float32)
    for flow in range(2):
        o = orders[flow]
        for q in range(2):
            second[flow][q].wait_recv()
        want = 1 - bits[o[2]]
        a1[flow, 2] = (a2[flow, want] + r1[flow, want].astype(jnp.float32)).astype(jnp.bfloat16)
        third[flow] = send(flow, 6, a1.at[flow, 2], r2.at[flow], o[2])
    for flow in range(2):
        o = orders[flow]
        keep = bits[o[2]]
        third[flow].wait_recv()
        out_ref[:, flow * half : (flow + 1) * half] = (
            a2[flow, keep] + r1[flow, keep].astype(jnp.float32) + r2[flow].astype(jnp.float32)
        ).astype(jnp.bfloat16)
    for flow in range(2):
        for copy in first[flow] + second[flow] + [third[flow]]:
            copy.wait_send()


def scattered(base, spot, back, parts):
    rows, width = base.shape
    own = width // parts
    half = own // 2
    return pl.pallas_call(
        scatter_kernel,
        out_shape=jax.ShapeDtypeStruct((rows, own), jnp.bfloat16),
        in_specs=[pl.BlockSpec(memory_space=pltpu.VMEM)] * 3,
        out_specs=pl.BlockSpec(memory_space=pltpu.VMEM),
        scratch_shapes=[
            pltpu.VMEM((2, 4, rows, half), jnp.bfloat16),
            pltpu.VMEM((2, 4, rows, half), jnp.bfloat16),
            pltpu.VMEM((2, 2, rows, half), jnp.bfloat16),
            pltpu.VMEM((2, rows, half), jnp.bfloat16),
            pltpu.VMEM((2, 3, rows, half), jnp.bfloat16),
            pltpu.VMEM((2, 2, rows, half), jnp.float32),
            pltpu.SemaphoreType.DMA((14,)),
            pltpu.SemaphoreType.DMA((14,)),
        ],
        compiler_params=pltpu.CompilerParams(
            collective_id=1, has_side_effects=True, vmem_limit_bytes=32 << 20
        ),
    )(base, spot, back)


def dispatch_kernel(n_dp, parts, x_ref, outgoing_ref, down_ref, w_ref, base_ref, coef_ref, held, total, send_sem, recv_sem):
    owners = n_dp * parts
    me = lax.axis_index("dp") * parts + lax.axis_index("tensor")

    def device(peer):
        return {"dp": peer // parts, "tensor": lax.rem(peer, parts)}

    barrier = pltpu.get_barrier_semaphore()
    for k in range(1, owners):
        peer = lax.rem(me + k, owners)
        pl.semaphore_signal(barrier, inc=1, device_id=device(peer), device_id_type=MESH)
    pl.semaphore_wait(barrier, owners - 1)
    copies = []
    for k in range(1, owners):
        peer = lax.rem(me + k, owners)
        copy = pltpu.make_async_remote_copy(
            src_ref=outgoing_ref.at[peer],
            dst_ref=held.at[k - 1],
            send_sem=send_sem.at[k - 1],
            recv_sem=recv_sem.at[k - 1],
            device_id=device(peer),
            device_id_type=MESH,
        )
        copy.start()
        copies.append(copy)
    rows, depth = x_ref.shape
    tile = 512

    def multiply(w_tile, base_tile):
        base_tile[...] = jnp.dot(x_ref[...], w_tile[...], preferred_element_type=jnp.float32)

    pltpu.emit_pipeline(
        multiply,
        grid=(w_ref.shape[1] // tile,),
        in_specs=[pl.BlockSpec((depth, tile), lambda j: (0, j))],
        out_specs=[pl.BlockSpec((rows, tile), lambda j: (0, j))],
    )(w_ref, base_ref)
    half = depth // 2
    lines = held.shape[1] // 2
    total[...] = jnp.zeros_like(total)
    for k in range(owners):
        source = lax.rem(me - k + owners, owners)
        part = lax.rem(source, parts)
        if k:
            copies[k - 1].wait_recv()
            rows_in = held[k - 1]
        else:
            rows_in = outgoing_ref[me]
        found = []
        for side in range(2):
            where = pl.ds(pl.multiple_of(part * depth + side * half, 128), half)
            found.append(
                lax.dot_general(
                    rows_in, down_ref[:, where], (((1,), (1,)), ((), ())), preferred_element_type=jnp.float32
                )
            )
        total[source // parts] += found[0][:lines] + found[1][lines:]
    coef_ref[...] = total[...]
    for copy in copies:
        copy.wait_send()


def dispatched(x, outgoing, down, w, n_dp, parts):
    owners, lines, half = outgoing.shape
    dma = pltpu.SemaphoreType.DMA((owners - 1,))
    return pl.pallas_call(
        functools.partial(dispatch_kernel, n_dp, parts),
        out_shape=(
            jax.ShapeDtypeStruct((x.shape[0], w.shape[1]), jnp.float32),
            jax.ShapeDtypeStruct((n_dp, lines // 2, down.shape[0]), jnp.float32),
        ),
        in_specs=[pl.BlockSpec(memory_space=pltpu.VMEM)] * 3 + [pl.BlockSpec(memory_space=pl.ANY)],
        out_specs=(pl.BlockSpec(memory_space=pl.ANY), pl.BlockSpec(memory_space=pltpu.VMEM)),
        scratch_shapes=[
            pltpu.VMEM((owners - 1, lines, half), jnp.bfloat16),
            pltpu.VMEM((n_dp, lines // 2, down.shape[0]), jnp.float32),
            dma,
            dma,
        ],
        compiler_params=pltpu.CompilerParams(
            collective_id=2, has_side_effects=True, vmem_limit_bytes=40 << 20
        ),
    )(x, outgoing, down, w)


def slots_of(index, owner_share, owners, capacity):
    streams = index.shape[0]
    owner = index // owner_share
    position = jnp.arange(streams, dtype=jnp.int32)
    before = (owner[:, None] == owner[None, :]) & (position[None, :] < position[:, None])
    slot = owner * capacity + jnp.sum(before.astype(jnp.int32), axis=1)
    return jnp.arange(owners * capacity, dtype=jnp.int32)[:, None] == slot[None, :]


def adapted(x, index, sibling_index, down_factor, up_factor, w, capacity, steps):
    n_dp = lax.axis_size("dp")
    parts = lax.axis_size("tensor")
    owners = n_dp * parts
    streams = index.shape[0]
    owner_share, channels, rank = down_factor.shape
    width = w.shape[1]
    group, mine = lax.axis_index("dp"), lax.axis_index("tensor")
    match = slots_of(index, owner_share, owners, capacity)
    same = jnp.eye(steps, dtype=jnp.bool_)
    spread_out = (
        match.reshape(owners, 1, capacity, 1, streams) & same[None, :, None, :, None]
    ).astype(jnp.bfloat16).reshape(owners, steps * capacity, steps * streams)
    flat = spread_out.reshape(owners * steps * capacity, steps * streams)
    half = x.shape[1] // 2
    sides = [
        jnp.dot(flat, x[:, side * half : (side + 1) * half], preferred_element_type=jnp.float32)
        .astype(jnp.bfloat16)
        .reshape(owners, steps * capacity, half)
        for side in range(2)
    ]
    outgoing = jnp.concatenate(sides, axis=1)
    down = jnp.transpose(down_factor, (0, 2, 1)).reshape(owner_share * rank, channels)
    base, coef = dispatched(x, outgoing, down, w, n_dp, parts)
    me = group * parts + mine
    keeps = []
    for source in range(n_dp):
        held = jnp.where(group == source, index, sibling_index)
        match_in = slots_of(held, owner_share, owners, capacity).reshape(owners, capacity, streams)
        match_in = lax.dynamic_index_in_dim(match_in, me, 0, keepdims=False)
        local = jnp.sum(jnp.where(match_in, (held % owner_share)[None, :], 0), axis=1)
        keep = local[:, None] == jnp.arange(owner_share, dtype=jnp.int32)[None, :]
        keeps.append(jnp.tile(jnp.repeat(keep, rank, axis=1), (steps, 1)))
    coeffs = jnp.where(jnp.stack(keeps), coef, 0.0).astype(jnp.bfloat16)
    delta = jnp.dot(
        coeffs.reshape(n_dp * steps * capacity, owner_share * rank),
        up_factor.reshape(owner_share * rank, width),
        preferred_element_type=jnp.float32,
    ).astype(jnp.bfloat16)
    delta = delta.reshape(n_dp, steps * capacity, width)
    back = lax.all_to_all(delta, "dp", split_axis=0, concat_axis=0, tiled=True)
    spot = lax.dynamic_index_in_dim(
        spread_out.reshape(n_dp, parts, steps * capacity, steps * streams), mine, 1, keepdims=False
    ).reshape(n_dp * steps * capacity, steps * streams).T
    total = scattered(base, spot, back.reshape(n_dp * steps * capacity, width), parts)
    return jnp.transpose(total.reshape(steps, streams, width // parts), (1, 0, 2))


def body(
    convolution_branch_input,
    gate_branch_input,
    convolution_state,
    initial_hidden_state,
    stream_adapter_index,
    convolution_weight,
    convolution_bias,
    input_coefficient_projection,
    step_size_norm_gain,
    step_size_projection,
    step_size_bias,
    negated_diagonal,
    channel_skip_gain,
    output_projection,
    adapter_down_factor,
    adapter_up_factor,
):
    n_dp = lax.axis_size("dp")
    tensor_parts = lax.axis_size("tensor")
    owners = n_dp * tensor_parts
    streams, steps, channel_count = convolution_branch_input.shape
    dt_rank = step_size_norm_gain.shape[0]
    states = negated_diagonal.shape[0]
    kernel = convolution_weight.shape[0]
    width = output_projection.shape[1]
    slice_part = width // tensor_parts
    owner_share = adapter_down_factor.shape[0]
    rank_width = adapter_down_factor.shape[2]
    capacity = max(2, 2 * streams // owners)
    full = jnp.concatenate([convolution_state, convolution_branch_input], axis=1)
    state = initial_hidden_state
    gathered = []
    conv_outs = []
    for step in range(steps):
        window = full[:, step : step + kernel].astype(jnp.float32)
        mixed = jnp.sum(window * convolution_weight[None], axis=1) + convolution_bias
        conv_outs.append(jax.nn.silu(mixed))
    conv_low = jnp.concatenate(conv_outs, axis=0).astype(jnp.bfloat16)
    partial_proj = jnp.dot(
        conv_low, input_coefficient_projection, preferred_element_type=jnp.float32
    )
    small = tensor_parts == 8 and n_dp == 2
    if small:
        dt_all, coef_all = summed_and_normed(
            partial_proj, step_size_norm_gain, tensor_parts, dt_rank
        )
    else:
        projected = lax.psum(partial_proj, "tensor")
        dt_raw = projected[:, :dt_rank]
        factor = lax.rsqrt(jnp.mean(dt_raw * dt_raw, axis=1, keepdims=True) + 1e-06)
        dt_all = (dt_raw * factor * step_size_norm_gain).astype(jnp.bfloat16)
        coef_all = projected[:, dt_rank:]
    for step in range(steps):
        conv_out = conv_outs[step]
        dt_low = dt_all[step * streams : (step + 1) * streams]
        coef = coef_all[step * streams : (step + 1) * streams]
        in_coef = coef[:, :states]
        out_coef = coef[:, states:]
        step_size = jax.nn.softplus(
            jnp.dot(dt_low, step_size_projection, preferred_element_type=jnp.float32)
            + step_size_bias
        )
        decay = jnp.exp(-step_size[:, None, :] * negated_diagonal[None])
        state = decay * state + step_size[:, None, :] * in_coef[:, :, None] * conv_out[:, None, :]
        read = jnp.sum(state * out_coef[:, :, None], axis=1) + channel_skip_gain * conv_out
        gated = read * jax.nn.silu(gate_branch_input[:, step].astype(jnp.float32))
        gathered.append(gated.astype(jnp.bfloat16))
    if small:
        sibling_index = lax.ppermute(stream_adapter_index, "dp", ((0, 1), (1, 0)))
        layer_out = adapted(
            jnp.concatenate(gathered, axis=0),
            stream_adapter_index,
            sibling_index,
            adapter_down_factor,
            adapter_up_factor,
            output_projection,
            capacity,
            steps,
        )
        return (layer_out, state)
    inner_y = jnp.stack(gathered, axis=1)
    owner = stream_adapter_index // owner_share
    local = stream_adapter_index % owner_share
    position = jnp.arange(streams, dtype=jnp.int32)
    before = (owner[:, None] == owner[None, :]) & (position[None, :] < position[:, None])
    current_tally = jnp.sum(before.astype(jnp.int32), axis=1)
    slot = owner * capacity + current_tally
    match = jnp.arange(owners * capacity, dtype=jnp.int32)[:, None] == slot[None, :]
    dispatch = match.astype(jnp.bfloat16)
    slot_local = jnp.sum(jnp.where(match, local[None, :], 0), axis=1).reshape(owners, capacity)
    outgoing = jnp.dot(
        dispatch,
        inner_y.reshape(streams, steps * channel_count),
        preferred_element_type=jnp.float32,
    )
    outgoing = outgoing.astype(jnp.bfloat16).reshape(owners, capacity, steps, channel_count)
    down_factor = adapter_down_factor.reshape(owner_share, tensor_parts, channel_count, rank_width)
    rows = lax.all_to_all(outgoing, ("dp", "tensor"), split_axis=0, concat_axis=0, tiled=True)
    idents = lax.all_to_all(slot_local, ("dp", "tensor"), split_axis=0, concat_axis=0, tiled=True)
    count = rows.shape[1]
    rows = rows.reshape(n_dp, tensor_parts, count, steps, channel_count)
    which = idents.reshape(n_dp, tensor_parts, count)[:, 0]
    select = (which[..., None] == jnp.arange(owner_share, dtype=jnp.int32)).astype(jnp.float32)
    every = jnp.einsum("itksc,atcr->iksar", rows, down_factor, preferred_element_type=jnp.float32)
    coeffs = jnp.einsum("iksar,ika->iksr", every, select).astype(jnp.bfloat16)
    up_factor_split = adapter_up_factor.reshape(owner_share, rank_width, tensor_parts, slice_part)
    spread = jnp.einsum(
        "iksr,arjc->ijksac", coeffs, up_factor_split, preferred_element_type=jnp.float32
    )
    delta = jnp.einsum("ijksac,ika->ijksc", spread, select).astype(jnp.bfloat16)
    delta = delta.reshape(owners, count, steps, slice_part)
    back = lax.all_to_all(delta, ("dp", "tensor"), split_axis=0, concat_axis=0, tiled=True)
    flat_rows = inner_y.reshape(streams * steps, channel_count)
    partial_value = jnp.dot(flat_rows, output_projection, preferred_element_type=jnp.float32)
    total = lax.psum_scatter(
        partial_value.reshape(streams, steps, width), "tensor", scatter_dimension=2, tiled=True
    )
    carried = jnp.dot(
        dispatch.T,
        back.reshape(owners * capacity, steps * slice_part),
        preferred_element_type=jnp.float32,
    )
    layer_out = (total + carried.reshape(streams, steps, slice_part)).astype(jnp.bfloat16)
    return (layer_out, state)


def solution(mesh):
    placed = (
        P(("groups", "dp"), None, "tensor"),
        P(("groups", "dp"), None, "tensor"),
        P(("groups", "dp"), None, "tensor"),
        P(("groups", "dp"), None, "tensor"),
        P(("groups", "dp")),
        P(None, "tensor"),
        P("tensor"),
        P("tensor", None),
        P(),
        P(None, "tensor"),
        P("tensor"),
        P(None, "tensor"),
        P("tensor"),
        P("tensor", None),
        P(("dp", "tensor"), None, None),
        P(("dp", "tensor"), None, None),
    )
    return jax.shard_map(
        body,
        mesh=mesh,
        in_specs=placed,
        out_specs=(P(("groups", "dp"), None, "tensor"), P(("groups", "dp"), None, "tensor")),
        check_vma=False,
    )
```

```python
import functools

import jax
import jax.numpy as jnp
from jax import lax
from jax.experimental import pallas as pl
from jax.experimental.pallas import tpu as pltpu
from jax.sharding import PartitionSpec as P

MESH = pl.DeviceIdType.MESH


def norm_kernel(parts, dt_rank, part_ref, gain_ref, dt_ref, coef_ref, held, send_sem, recv_sem, send2, recv2, send3, recv3):
    me = lax.axis_index("tensor")
    barrier = pltpu.get_barrier_semaphore()
    for k in range(1, parts):
        peer = lax.rem(me + k, parts)
        pl.semaphore_signal(barrier, inc=1, device_id={"tensor": peer}, device_id_type=MESH)
    pl.semaphore_wait(barrier, parts - 1)
    copies = []
    for k in range(1, parts):
        peer = lax.rem(me + k, parts)
        copy = pltpu.make_async_remote_copy(
            src_ref=part_ref.at[peer],
            dst_ref=held.at[k - 1],
            send_sem=send_sem.at[k - 1],
            recv_sem=recv_sem.at[k - 1],
            device_id={"tensor": peer},
            device_id_type=MESH,
        )
        copy.start()
        copies.append(copy)
    total = part_ref[me]
    for k in range(1, parts):
        copies[k - 1].wait_recv()
        total = total + held[k - 1]
    dt_raw = total[:, :dt_rank]
    factor = lax.rsqrt(jnp.mean(dt_raw * dt_raw, axis=1, keepdims=True) + 1e-06)
    dt_low = dt_raw * factor * gain_ref[...]
    rows = dt_low.shape[0]
    padded = dt_ref.shape[1]
    if padded > rows:
        dt_low = jnp.concatenate([dt_low, jnp.zeros((padded - rows, dt_rank), jnp.float32)], axis=0)
    dt_ref[me] = dt_low.astype(jnp.bfloat16)
    coef_ref[me] = total[:, dt_rank:]
    later = []
    for k in range(1, parts):
        peer = lax.rem(me + k, parts)
        for ref, out_sem, in_sem in ((dt_ref, send2, recv2), (coef_ref, send3, recv3)):
            copy = pltpu.make_async_remote_copy(
                src_ref=ref.at[me],
                dst_ref=ref.at[me],
                send_sem=out_sem.at[k - 1],
                recv_sem=in_sem.at[k - 1],
                device_id={"tensor": peer},
                device_id_type=MESH,
            )
            copy.start()
            later.append(copy)
    for copy in copies:
        copy.wait_send()
    for copy in later:
        copy.wait()


def summed_and_normed(partial, gain, parts, dt_rank):
    rows, columns = partial.shape
    share = rows // parts
    padded = -(-share // 16) * 16
    dma = pltpu.SemaphoreType.DMA((parts - 1,))
    dt, coef = pl.pallas_call(
        functools.partial(norm_kernel, parts, dt_rank),
        out_shape=(
            jax.ShapeDtypeStruct((parts, padded, dt_rank), jnp.bfloat16),
            jax.ShapeDtypeStruct((parts, share, columns - dt_rank), jnp.float32),
        ),
        in_specs=[pl.BlockSpec(memory_space=pltpu.VMEM)] * 2,
        out_specs=(pl.BlockSpec(memory_space=pltpu.VMEM),) * 2,
        scratch_shapes=[
            pltpu.VMEM((parts - 1, share, columns), jnp.float32),
        ]
        + [dma] * 6,
        compiler_params=pltpu.CompilerParams(
            collective_id=0, has_side_effects=True, vmem_limit_bytes=24 << 20
        ),
    )(partial.reshape(parts, share, columns), gain.reshape(1, dt_rank))
    return dt[:, :share].reshape(rows, dt_rank), coef.reshape(rows, columns - dt_rank)


CHUNKS = 2


def scatter_kernel(base_ref, spot_ref, back_ref, out_ref, *scratch):
    held = (scratch[0:6], scratch[6:12])
    send_sem, recv_sem = scratch[12:]
    me = lax.axis_index("tensor")
    y, z = lax.rem(me, 2), me // 2
    h = z // 2
    c = lax.rem(z + h, 2)
    bits = (y, c, h)

    def place(sel):
        far = sel[1] + sel[2] * (3 - 2 * sel[1])
        return far * 2 + sel[0]

    def flipped(d):
        return tuple(1 - b if i == d else b for i, b in enumerate(bits))

    barrier = pltpu.get_barrier_semaphore()
    for d in range(3):
        pl.semaphore_signal(barrier, inc=1, device_id={"tensor": place(flipped(d))}, device_id_type=MESH)
    pl.semaphore_wait(barrier, 3)
    rows, width = out_ref.shape
    lines = rows // CHUNKS
    starts, sizes = (0, 3 * width // 4), (3 * width // 4, width // 4)
    orders = ((0, 1, 2), (1, 0, 2))
    units = [(chunk, flow) for chunk in range(CHUNKS) for flow in range(2)]

    def send(unit, n, src, dst, d):
        at = (unit[0] * 2 + unit[1]) * 7 + n
        copy = pltpu.make_async_remote_copy(
            src_ref=src,
            dst_ref=dst,
            send_sem=send_sem.at[at],
            recv_sem=recv_sem.at[at],
            device_id={"tensor": place(flipped(d))},
            device_id_type=MESH,
        )
        copy.start()
        return copy

    def block(unit, sel):
        chunk, flow = unit
        part = pl.ds(chunk * lines, lines)
        where = pl.ds(pl.multiple_of(place(sel) * width + starts[flow], 128), sizes[flow])
        extra = jnp.dot(spot_ref[part, :], back_ref[:, where], preferred_element_type=jnp.float32)
        return base_ref[part, where] + extra

    def chosen(order, values):
        sel = [None] * 3
        for d, v in zip(order, values):
            sel[d] = v
        return tuple(sel)

    first = {unit: [] for unit in units}
    second = {unit: [] for unit in units}
    third = {}
    for unit in units:
        chunk, flow = unit
        x_ref, r0 = held[flow][0], held[flow][1]
        o = orders[flow]
        for p in range(2):
            b1 = 1 - bits[o[1]] if p == 0 else bits[o[1]]
            for q in range(2):
                n = p * 2 + q
                sel = chosen(o, (1 - bits[o[0]], b1, q))
                x_ref[chunk, n] = block(unit, sel).astype(jnp.bfloat16)
                first[unit].append(send(unit, n, x_ref.at[chunk, n], r0.at[chunk, n], o[0]))
    for unit in units:
        chunk, flow = unit
        x_ref, r0, r1, r2, a1, a2 = held[flow]
        o = orders[flow]
        for q in range(2):
            sel = chosen(o, (bits[o[0]], 1 - bits[o[1]], q))
            own = block(unit, sel)
            first[unit][q].wait_recv()
            a1[chunk, q] = (own + r0[chunk, q].astype(jnp.float32)).astype(jnp.bfloat16)
            second[unit].append(send(unit, 4 + q, a1.at[chunk, q], r1.at[chunk, q], o[1]))
        for q in range(2):
            sel = chosen(o, (bits[o[0]], bits[o[1]], q))
            own = block(unit, sel)
            first[unit][2 + q].wait_recv()
            a2[chunk, q] = own + r0[chunk, 2 + q].astype(jnp.float32)
    for unit in units:
        chunk, flow = unit
        x_ref, r0, r1, r2, a1, a2 = held[flow]
        for q in range(2):
            second[unit][q].wait_recv()
        want = 1 - bits[2]
        a1[chunk, 2] = (a2[chunk, want] + r1[chunk, want].astype(jnp.float32)).astype(jnp.bfloat16)
        third[unit] = send(unit, 6, a1.at[chunk, 2], r2.at[chunk], 2)
    for unit in units:
        chunk, flow = unit
        x_ref, r0, r1, r2, a1, a2 = held[flow]
        keep = bits[2]
        third[unit].wait_recv()
        out_ref[chunk * lines : (chunk + 1) * lines, starts[flow] : starts[flow] + sizes[flow]] = (
            a2[chunk, keep] + r1[chunk, keep].astype(jnp.float32) + r2[chunk].astype(jnp.float32)
        ).astype(jnp.bfloat16)
    for unit in units:
        for copy in first[unit] + second[unit] + [third[unit]]:
            copy.wait_send()


def scattered(base, spot, back, parts):
    rows, width = base.shape
    own = width // parts
    lines = rows // CHUNKS
    buffers = []
    for size in (3 * own // 4, own // 4):
        for shape, dtype in (
            ((CHUNKS, 4, lines, size), jnp.bfloat16),
            ((CHUNKS, 4, lines, size), jnp.bfloat16),
            ((CHUNKS, 2, lines, size), jnp.bfloat16),
            ((CHUNKS, lines, size), jnp.bfloat16),
            ((CHUNKS, 3, lines, size), jnp.bfloat16),
            ((CHUNKS, 2, lines, size), jnp.float32),
        ):
            buffers.append(pltpu.VMEM(shape, dtype))
    dma = pltpu.SemaphoreType.DMA((14 * CHUNKS,))
    return pl.pallas_call(
        scatter_kernel,
        out_shape=jax.ShapeDtypeStruct((rows, own), jnp.bfloat16),
        in_specs=[pl.BlockSpec(memory_space=pltpu.VMEM)] * 3,
        out_specs=pl.BlockSpec(memory_space=pltpu.VMEM),
        scratch_shapes=buffers + [dma, dma],
        compiler_params=pltpu.CompilerParams(
            collective_id=1, has_side_effects=True, vmem_limit_bytes=32 << 20
        ),
    )(base, spot, back)


def dispatch_kernel(n_dp, parts, x_ref, outgoing_ref, down_ref, w_ref, base_ref, coef_ref, held, total, send_sem, recv_sem):
    owners = n_dp * parts
    me = lax.axis_index("dp") * parts + lax.axis_index("tensor")

    def device(peer):
        return {"dp": peer // parts, "tensor": lax.rem(peer, parts)}

    barrier = pltpu.get_barrier_semaphore()
    for k in range(1, owners):
        peer = lax.rem(me + k, owners)
        pl.semaphore_signal(barrier, inc=1, device_id=device(peer), device_id_type=MESH)
    pl.semaphore_wait(barrier, owners - 1)
    copies = []
    for k in range(1, owners):
        peer = lax.rem(me + k, owners)
        copy = pltpu.make_async_remote_copy(
            src_ref=outgoing_ref.at[peer],
            dst_ref=held.at[k - 1],
            send_sem=send_sem.at[k - 1],
            recv_sem=recv_sem.at[k - 1],
            device_id=device(peer),
            device_id_type=MESH,
        )
        copy.start()
        copies.append(copy)
    rows, depth = x_ref.shape
    tile = 512

    def multiply(w_tile, base_tile):
        base_tile[...] = jnp.dot(x_ref[...], w_tile[...], preferred_element_type=jnp.float32)

    pltpu.emit_pipeline(
        multiply,
        grid=(w_ref.shape[1] // tile,),
        in_specs=[pl.BlockSpec((depth, tile), lambda j: (0, j))],
        out_specs=[pl.BlockSpec((rows, tile), lambda j: (0, j))],
    )(w_ref, base_ref)
    half = depth // 2
    lines = held.shape[1] // 2
    total[...] = jnp.zeros_like(total)
    for k in range(owners):
        source = lax.rem(me - k + owners, owners)
        part = lax.rem(source, parts)
        if k:
            copies[k - 1].wait_recv()
            rows_in = held[k - 1]
        else:
            rows_in = outgoing_ref[me]
        found = []
        for side in range(2):
            where = pl.ds(pl.multiple_of(part * depth + side * half, 128), half)
            found.append(
                lax.dot_general(
                    rows_in, down_ref[:, where], (((1,), (1,)), ((), ())), preferred_element_type=jnp.float32
                )
            )
        total[source // parts] += found[0][:lines] + found[1][lines:]
    coef_ref[...] = total[...]
    for copy in copies:
        copy.wait_send()


def dispatched(x, outgoing, down, w, n_dp, parts):
    owners, lines, half = outgoing.shape
    dma = pltpu.SemaphoreType.DMA((owners - 1,))
    return pl.pallas_call(
        functools.partial(dispatch_kernel, n_dp, parts),
        out_shape=(
            jax.ShapeDtypeStruct((x.shape[0], w.shape[1]), jnp.float32),
            jax.ShapeDtypeStruct((n_dp, lines // 2, down.shape[0]), jnp.float32),
        ),
        in_specs=[pl.BlockSpec(memory_space=pltpu.VMEM)] * 3 + [pl.BlockSpec(memory_space=pl.ANY)],
        out_specs=(pl.BlockSpec(memory_space=pl.ANY), pl.BlockSpec(memory_space=pltpu.VMEM)),
        scratch_shapes=[
            pltpu.VMEM((owners - 1, lines, half), jnp.bfloat16),
            pltpu.VMEM((n_dp, lines // 2, down.shape[0]), jnp.float32),
            dma,
            dma,
        ],
        compiler_params=pltpu.CompilerParams(
            collective_id=2, has_side_effects=True, vmem_limit_bytes=40 << 20
        ),
    )(x, outgoing, down, w)


def slots_of(index, owner_share, owners, capacity):
    streams = index.shape[0]
    owner = index // owner_share
    position = jnp.arange(streams, dtype=jnp.int32)
    before = (owner[:, None] == owner[None, :]) & (position[None, :] < position[:, None])
    slot = owner * capacity + jnp.sum(before.astype(jnp.int32), axis=1)
    return jnp.arange(owners * capacity, dtype=jnp.int32)[:, None] == slot[None, :]


def adapted(x, index, sibling_index, down_factor, up_factor, w, capacity, steps):
    n_dp = lax.axis_size("dp")
    parts = lax.axis_size("tensor")
    owners = n_dp * parts
    streams = index.shape[0]
    owner_share, channels, rank = down_factor.shape
    width = w.shape[1]
    group, mine = lax.axis_index("dp"), lax.axis_index("tensor")
    match = slots_of(index, owner_share, owners, capacity)
    same = jnp.eye(steps, dtype=jnp.bool_)
    spread_out = (
        match.reshape(owners, 1, capacity, 1, streams) & same[None, :, None, :, None]
    ).astype(jnp.bfloat16).reshape(owners, steps * capacity, steps * streams)
    flat = spread_out.reshape(owners * steps * capacity, steps * streams)
    half = x.shape[1] // 2
    sides = [
        jnp.dot(flat, x[:, side * half : (side + 1) * half], preferred_element_type=jnp.float32)
        .astype(jnp.bfloat16)
        .reshape(owners, steps * capacity, half)
        for side in range(2)
    ]
    outgoing = jnp.concatenate(sides, axis=1)
    down = jnp.transpose(down_factor, (0, 2, 1)).reshape(owner_share * rank, channels)
    base, coef = dispatched(x, outgoing, down, w, n_dp, parts)
    me = group * parts + mine
    keeps = []
    for source in range(n_dp):
        held = jnp.where(group == source, index, sibling_index)
        match_in = slots_of(held, owner_share, owners, capacity).reshape(owners, capacity, streams)
        match_in = lax.dynamic_index_in_dim(match_in, me, 0, keepdims=False)
        local = jnp.sum(jnp.where(match_in, (held % owner_share)[None, :], 0), axis=1)
        keep = local[:, None] == jnp.arange(owner_share, dtype=jnp.int32)[None, :]
        keeps.append(jnp.tile(jnp.repeat(keep, rank, axis=1), (steps, 1)))
    coeffs = jnp.where(jnp.stack(keeps), coef, 0.0).astype(jnp.bfloat16)
    delta = jnp.dot(
        coeffs.reshape(n_dp * steps * capacity, owner_share * rank),
        up_factor.reshape(owner_share * rank, width),
        preferred_element_type=jnp.float32,
    ).astype(jnp.bfloat16)
    delta = delta.reshape(n_dp, steps * capacity, width)
    back = lax.all_to_all(delta, "dp", split_axis=0, concat_axis=0, tiled=True)
    spot = lax.dynamic_index_in_dim(
        spread_out.reshape(n_dp, parts, steps * capacity, steps * streams), mine, 1, keepdims=False
    ).reshape(n_dp * steps * capacity, steps * streams).T
    total = scattered(base, spot, back.reshape(n_dp * steps * capacity, width), parts)
    return jnp.transpose(total.reshape(steps, streams, width // parts), (1, 0, 2))


def body(
    convolution_branch_input,
    gate_branch_input,
    convolution_state,
    initial_hidden_state,
    stream_adapter_index,
    convolution_weight,
    convolution_bias,
    input_coefficient_projection,
    step_size_norm_gain,
    step_size_projection,
    step_size_bias,
    negated_diagonal,
    channel_skip_gain,
    output_projection,
    adapter_down_factor,
    adapter_up_factor,
):
    n_dp = lax.axis_size("dp")
    tensor_parts = lax.axis_size("tensor")
    owners = n_dp * tensor_parts
    streams, steps, channel_count = convolution_branch_input.shape
    dt_rank = step_size_norm_gain.shape[0]
    states = negated_diagonal.shape[0]
    kernel = convolution_weight.shape[0]
    width = output_projection.shape[1]
    slice_part = width // tensor_parts
    owner_share = adapter_down_factor.shape[0]
    rank_width = adapter_down_factor.shape[2]
    capacity = max(2, 2 * streams // owners)
    full = jnp.concatenate([convolution_state, convolution_branch_input], axis=1)
    state = initial_hidden_state
    gathered = []
    conv_outs = []
    for step in range(steps):
        window = full[:, step : step + kernel].astype(jnp.float32)
        mixed = jnp.sum(window * convolution_weight[None], axis=1) + convolution_bias
        conv_outs.append(jax.nn.silu(mixed))
    conv_low = jnp.concatenate(conv_outs, axis=0).astype(jnp.bfloat16)
    partial_proj = jnp.dot(
        conv_low, input_coefficient_projection, preferred_element_type=jnp.float32
    )
    small = tensor_parts == 8 and n_dp == 2
    if small:
        dt_all, coef_all = summed_and_normed(
            partial_proj, step_size_norm_gain, tensor_parts, dt_rank
        )
    else:
        projected = lax.psum(partial_proj, "tensor")
        dt_raw = projected[:, :dt_rank]
        factor = lax.rsqrt(jnp.mean(dt_raw * dt_raw, axis=1, keepdims=True) + 1e-06)
        dt_all = (dt_raw * factor * step_size_norm_gain).astype(jnp.bfloat16)
        coef_all = projected[:, dt_rank:]
    for step in range(steps):
        conv_out = conv_outs[step]
        dt_low = dt_all[step * streams : (step + 1) * streams]
        coef = coef_all[step * streams : (step + 1) * streams]
        in_coef = coef[:, :states]
        out_coef = coef[:, states:]
        step_size = jax.nn.softplus(
            jnp.dot(dt_low, step_size_projection, preferred_element_type=jnp.float32)
            + step_size_bias
        )
        decay = jnp.exp(-step_size[:, None, :] * negated_diagonal[None])
        state = decay * state + step_size[:, None, :] * in_coef[:, :, None] * conv_out[:, None, :]
        read = jnp.sum(state * out_coef[:, :, None], axis=1) + channel_skip_gain * conv_out
        gated = read * jax.nn.silu(gate_branch_input[:, step].astype(jnp.float32))
        gathered.append(gated.astype(jnp.bfloat16))
    if small:
        sibling_index = lax.ppermute(stream_adapter_index, "dp", ((0, 1), (1, 0)))
        layer_out = adapted(
            jnp.concatenate(gathered, axis=0),
            stream_adapter_index,
            sibling_index,
            adapter_down_factor,
            adapter_up_factor,
            output_projection,
            capacity,
            steps,
        )
        return (layer_out, state)
    inner_y = jnp.stack(gathered, axis=1)
    owner = stream_adapter_index // owner_share
    local = stream_adapter_index % owner_share
    position = jnp.arange(streams, dtype=jnp.int32)
    before = (owner[:, None] == owner[None, :]) & (position[None, :] < position[:, None])
    current_tally = jnp.sum(before.astype(jnp.int32), axis=1)
    slot = owner * capacity + current_tally
    match = jnp.arange(owners * capacity, dtype=jnp.int32)[:, None] == slot[None, :]
    dispatch = match.astype(jnp.bfloat16)
    slot_local = jnp.sum(jnp.where(match, local[None, :], 0), axis=1).reshape(owners, capacity)
    outgoing = jnp.dot(
        dispatch,
        inner_y.reshape(streams, steps * channel_count),
        preferred_element_type=jnp.float32,
    )
    outgoing = outgoing.astype(jnp.bfloat16).reshape(owners, capacity, steps, channel_count)
    down_factor = adapter_down_factor.reshape(owner_share, tensor_parts, channel_count, rank_width)
    rows = lax.all_to_all(outgoing, ("dp", "tensor"), split_axis=0, concat_axis=0, tiled=True)
    idents = lax.all_to_all(slot_local, ("dp", "tensor"), split_axis=0, concat_axis=0, tiled=True)
    count = rows.shape[1]
    rows = rows.reshape(n_dp, tensor_parts, count, steps, channel_count)
    which = idents.reshape(n_dp, tensor_parts, count)[:, 0]
    select = (which[..., None] == jnp.arange(owner_share, dtype=jnp.int32)).astype(jnp.float32)
    every = jnp.einsum("itksc,atcr->iksar", rows, down_factor, preferred_element_type=jnp.float32)
    coeffs = jnp.einsum("iksar,ika->iksr", every, select).astype(jnp.bfloat16)
    up_factor_split = adapter_up_factor.reshape(owner_share, rank_width, tensor_parts, slice_part)
    spread = jnp.einsum(
        "iksr,arjc->ijksac", coeffs, up_factor_split, preferred_element_type=jnp.float32
    )
    delta = jnp.einsum("ijksac,ika->ijksc", spread, select).astype(jnp.bfloat16)
    delta = delta.reshape(owners, count, steps, slice_part)
    back = lax.all_to_all(delta, ("dp", "tensor"), split_axis=0, concat_axis=0, tiled=True)
    flat_rows = inner_y.reshape(streams * steps, channel_count)
    partial_value = jnp.dot(flat_rows, output_projection, preferred_element_type=jnp.float32)
    total = lax.psum_scatter(
        partial_value.reshape(streams, steps, width), "tensor", scatter_dimension=2, tiled=True
    )
    carried = jnp.dot(
        dispatch.T,
        back.reshape(owners * capacity, steps * slice_part),
        preferred_element_type=jnp.float32,
    )
    layer_out = (total + carried.reshape(streams, steps, slice_part)).astype(jnp.bfloat16)
    return (layer_out, state)


def solution(mesh):
    placed = (
        P(("groups", "dp"), None, "tensor"),
        P(("groups", "dp"), None, "tensor"),
        P(("groups", "dp"), None, "tensor"),
        P(("groups", "dp"), None, "tensor"),
        P(("groups", "dp")),
        P(None, "tensor"),
        P("tensor"),
        P("tensor", None),
        P(),
        P(None, "tensor"),
        P("tensor"),
        P(None, "tensor"),
        P("tensor"),
        P("tensor", None),
        P(("dp", "tensor"), None, None),
        P(("dp", "tensor"), None, None),
    )
    return jax.shard_map(
        body,
        mesh=mesh,
        in_specs=placed,
        out_specs=(P(("groups", "dp"), None, "tensor"), P(("groups", "dp"), None, "tensor")),
        check_vma=False,
    )
```

```python
import functools

import jax
import jax.numpy as jnp
from jax import lax
from jax.experimental import pallas as pl
from jax.experimental.pallas import tpu as pltpu
from jax.sharding import PartitionSpec as P

MESH = pl.DeviceIdType.MESH


def norm_kernel(parts, dt_rank, part_ref, gain_ref, dt_ref, coef_ref, held, send_sem, recv_sem, send2, recv2, send3, recv3):
    me = lax.axis_index("tensor")
    barrier = pltpu.get_barrier_semaphore()
    for k in range(1, parts):
        peer = lax.rem(me + k, parts)
        pl.semaphore_signal(barrier, inc=1, device_id={"tensor": peer}, device_id_type=MESH)
    pl.semaphore_wait(barrier, parts - 1)
    copies = []
    for k in range(1, parts):
        peer = lax.rem(me + k, parts)
        copy = pltpu.make_async_remote_copy(
            src_ref=part_ref.at[peer],
            dst_ref=held.at[k - 1],
            send_sem=send_sem.at[k - 1],
            recv_sem=recv_sem.at[k - 1],
            device_id={"tensor": peer},
            device_id_type=MESH,
        )
        copy.start()
        copies.append(copy)
    total = part_ref[me]
    for k in range(1, parts):
        copies[k - 1].wait_recv()
        total = total + held[k - 1]
    dt_raw = total[:, :dt_rank]
    factor = lax.rsqrt(jnp.mean(dt_raw * dt_raw, axis=1, keepdims=True) + 1e-06)
    dt_low = dt_raw * factor * gain_ref[...]
    rows = dt_low.shape[0]
    padded = dt_ref.shape[1]
    if padded > rows:
        dt_low = jnp.concatenate([dt_low, jnp.zeros((padded - rows, dt_rank), jnp.float32)], axis=0)
    dt_ref[me] = dt_low.astype(jnp.bfloat16)
    coef_ref[me] = total[:, dt_rank:]
    later = []
    for k in range(1, parts):
        peer = lax.rem(me + k, parts)
        for ref, out_sem, in_sem in ((dt_ref, send2, recv2), (coef_ref, send3, recv3)):
            copy = pltpu.make_async_remote_copy(
                src_ref=ref.at[me],
                dst_ref=ref.at[me],
                send_sem=out_sem.at[k - 1],
                recv_sem=in_sem.at[k - 1],
                device_id={"tensor": peer},
                device_id_type=MESH,
            )
            copy.start()
            later.append(copy)
    for copy in copies:
        copy.wait_send()
    for copy in later:
        copy.wait()


def summed_and_normed(partial, gain, parts, dt_rank):
    rows, columns = partial.shape
    share = rows // parts
    padded = -(-share // 16) * 16
    dma = pltpu.SemaphoreType.DMA((parts - 1,))
    dt, coef = pl.pallas_call(
        functools.partial(norm_kernel, parts, dt_rank),
        out_shape=(
            jax.ShapeDtypeStruct((parts, padded, dt_rank), jnp.bfloat16),
            jax.ShapeDtypeStruct((parts, share, columns - dt_rank), jnp.float32),
        ),
        in_specs=[pl.BlockSpec(memory_space=pltpu.VMEM)] * 2,
        out_specs=(pl.BlockSpec(memory_space=pltpu.VMEM),) * 2,
        scratch_shapes=[
            pltpu.VMEM((parts - 1, share, columns), jnp.float32),
        ]
        + [dma] * 6,
        compiler_params=pltpu.CompilerParams(
            collective_id=0, has_side_effects=True, vmem_limit_bytes=24 << 20
        ),
    )(partial.reshape(parts, share, columns), gain.reshape(1, dt_rank))
    return dt[:, :share].reshape(rows, dt_rank), coef.reshape(rows, columns - dt_rank)


CHUNKS = 2


def scatter_kernel(base_ref, spot_ref, back_ref, out_ref, *scratch):
    held = (scratch[0:6], scratch[6:12])
    send_sem, recv_sem = scratch[12:]
    me = lax.axis_index("tensor")
    y, z = lax.rem(me, 2), me // 2
    h = z // 2
    c = lax.rem(z + h, 2)
    bits = (y, c, h)

    def place(sel):
        far = sel[1] + sel[2] * (3 - 2 * sel[1])
        return far * 2 + sel[0]

    def flipped(d):
        return tuple(1 - b if i == d else b for i, b in enumerate(bits))

    barrier = pltpu.get_barrier_semaphore()
    for d in range(3):
        pl.semaphore_signal(barrier, inc=1, device_id={"tensor": place(flipped(d))}, device_id_type=MESH)
    pl.semaphore_wait(barrier, 3)
    rows, width = out_ref.shape
    lines = rows // CHUNKS
    starts, sizes = (0, 3 * width // 4), (3 * width // 4, width // 4)
    orders = ((0, 1, 2), (1, 0, 2))
    units = [(chunk, flow) for chunk in range(CHUNKS) for flow in range(2)]

    def send(unit, n, src, dst, d):
        at = (unit[0] * 2 + unit[1]) * 7 + n
        copy = pltpu.make_async_remote_copy(
            src_ref=src,
            dst_ref=dst,
            send_sem=send_sem.at[at],
            recv_sem=recv_sem.at[at],
            device_id={"tensor": place(flipped(d))},
            device_id_type=MESH,
        )
        copy.start()
        return copy

    def block(unit, sel):
        chunk, flow = unit
        part = pl.ds(chunk * lines, lines)
        where = pl.ds(pl.multiple_of(place(sel) * width + starts[flow], 128), sizes[flow])
        extra = jnp.dot(spot_ref[part, :], back_ref[:, where], preferred_element_type=jnp.float32)
        return base_ref[part, where] + extra

    def chosen(order, values):
        sel = [None] * 3
        for d, v in zip(order, values):
            sel[d] = v
        return tuple(sel)

    first = {unit: [] for unit in units}
    second = {unit: [] for unit in units}
    third = {}
    for unit in units:
        chunk, flow = unit
        x_ref, r0 = held[flow][0], held[flow][1]
        o = orders[flow]
        for p in range(2):
            b1 = 1 - bits[o[1]] if p == 0 else bits[o[1]]
            for q in range(2):
                n = p * 2 + q
                sel = chosen(o, (1 - bits[o[0]], b1, q))
                x_ref[chunk, n] = block(unit, sel).astype(jnp.bfloat16)
                first[unit].append(send(unit, n, x_ref.at[chunk, n], r0.at[chunk, n], o[0]))
    for unit in units:
        chunk, flow = unit
        x_ref, r0, r1, r2, a1, a2 = held[flow]
        o = orders[flow]
        for q in range(2):
            sel = chosen(o, (bits[o[0]], 1 - bits[o[1]], q))
            own = block(unit, sel)
            first[unit][q].wait_recv()
            a1[chunk, q] = (own + r0[chunk, q].astype(jnp.float32)).astype(jnp.bfloat16)
            second[unit].append(send(unit, 4 + q, a1.at[chunk, q], r1.at[chunk, q], o[1]))
        for q in range(2):
            sel = chosen(o, (bits[o[0]], bits[o[1]], q))
            own = block(unit, sel)
            first[unit][2 + q].wait_recv()
            a2[chunk, q] = own + r0[chunk, 2 + q].astype(jnp.float32)
    for unit in units:
        chunk, flow = unit
        x_ref, r0, r1, r2, a1, a2 = held[flow]
        for q in range(2):
            second[unit][q].wait_recv()
        want = 1 - bits[2]
        a1[chunk, 2] = (a2[chunk, want] + r1[chunk, want].astype(jnp.float32)).astype(jnp.bfloat16)
        third[unit] = send(unit, 6, a1.at[chunk, 2], r2.at[chunk], 2)
    for unit in units:
        chunk, flow = unit
        x_ref, r0, r1, r2, a1, a2 = held[flow]
        keep = bits[2]
        third[unit].wait_recv()
        out_ref[chunk * lines : (chunk + 1) * lines, starts[flow] : starts[flow] + sizes[flow]] = (
            a2[chunk, keep] + r1[chunk, keep].astype(jnp.float32) + r2[chunk].astype(jnp.float32)
        ).astype(jnp.bfloat16)
    for unit in units:
        for copy in first[unit] + second[unit] + [third[unit]]:
            copy.wait_send()


def scattered(base, spot, back, parts):
    rows, width = base.shape
    own = width // parts
    lines = rows // CHUNKS
    buffers = []
    for size in (3 * own // 4, own // 4):
        for shape, dtype in (
            ((CHUNKS, 4, lines, size), jnp.bfloat16),
            ((CHUNKS, 4, lines, size), jnp.bfloat16),
            ((CHUNKS, 2, lines, size), jnp.bfloat16),
            ((CHUNKS, lines, size), jnp.bfloat16),
            ((CHUNKS, 3, lines, size), jnp.bfloat16),
            ((CHUNKS, 2, lines, size), jnp.float32),
        ):
            buffers.append(pltpu.VMEM(shape, dtype))
    dma = pltpu.SemaphoreType.DMA((14 * CHUNKS,))
    return pl.pallas_call(
        scatter_kernel,
        out_shape=jax.ShapeDtypeStruct((rows, own), jnp.bfloat16),
        in_specs=[pl.BlockSpec(memory_space=pltpu.VMEM)] * 3,
        out_specs=pl.BlockSpec(memory_space=pltpu.VMEM),
        scratch_shapes=buffers + [dma, dma],
        compiler_params=pltpu.CompilerParams(
            collective_id=1, has_side_effects=True, vmem_limit_bytes=32 << 20
        ),
    )(base, spot, back)


def dispatch_kernel(n_dp, parts, x_ref, outgoing_ref, down_ref, w_ref, base_ref, coef_ref, held, total, down_here, down_sem, send_sem, recv_sem):
    owners = n_dp * parts
    fetch = pltpu.make_async_copy(down_ref, down_here, down_sem)
    fetch.start()
    me = lax.axis_index("dp") * parts + lax.axis_index("tensor")

    def device(peer):
        return {"dp": peer // parts, "tensor": lax.rem(peer, parts)}

    barrier = pltpu.get_barrier_semaphore()
    for k in range(1, owners):
        peer = lax.rem(me + k, owners)
        pl.semaphore_signal(barrier, inc=1, device_id=device(peer), device_id_type=MESH)
    pl.semaphore_wait(barrier, owners - 1)
    copies = []
    for k in range(1, owners):
        peer = lax.rem(me + k, owners)
        copy = pltpu.make_async_remote_copy(
            src_ref=outgoing_ref.at[peer],
            dst_ref=held.at[k - 1],
            send_sem=send_sem.at[k - 1],
            recv_sem=recv_sem.at[k - 1],
            device_id=device(peer),
            device_id_type=MESH,
        )
        copy.start()
        copies.append(copy)
    rows, depth = x_ref.shape
    tile = 512

    def multiply(w_tile, base_tile):
        base_tile[...] = jnp.dot(x_ref[...], w_tile[...], preferred_element_type=jnp.float32)

    pltpu.emit_pipeline(
        multiply,
        grid=(w_ref.shape[1] // tile,),
        in_specs=[pl.BlockSpec((depth, tile), lambda j: (0, j))],
        out_specs=[pl.BlockSpec((rows, tile), lambda j: (0, j))],
    )(w_ref, base_ref)
    half = depth // 2
    lines = held.shape[1] // 2
    total[...] = jnp.zeros_like(total)
    fetch.wait()
    for k in range(owners):
        source = lax.rem(me - k + owners, owners)
        part = lax.rem(source, parts)
        if k:
            copies[k - 1].wait_recv()
            rows_in = held[k - 1]
        else:
            rows_in = outgoing_ref[me]
        found = []
        for side in range(2):
            where = pl.ds(pl.multiple_of(part * depth + side * half, 128), half)
            found.append(
                lax.dot_general(
                    rows_in, down_here[:, where], (((1,), (1,)), ((), ())), preferred_element_type=jnp.float32
                )
            )
        total[source // parts] += found[0][:lines] + found[1][lines:]
    coef_ref[...] = total[...]
    for copy in copies:
        copy.wait_send()


def dispatched(x, outgoing, down, w, n_dp, parts):
    owners, lines, half = outgoing.shape
    dma = pltpu.SemaphoreType.DMA((owners - 1,))
    return pl.pallas_call(
        functools.partial(dispatch_kernel, n_dp, parts),
        out_shape=(
            jax.ShapeDtypeStruct((x.shape[0], w.shape[1]), jnp.float32),
            jax.ShapeDtypeStruct((n_dp, lines // 2, down.shape[0]), jnp.float32),
        ),
        in_specs=[pl.BlockSpec(memory_space=pltpu.VMEM)] * 2 + [pl.BlockSpec(memory_space=pl.ANY)] * 2,
        out_specs=(pl.BlockSpec(memory_space=pl.ANY), pl.BlockSpec(memory_space=pltpu.VMEM)),
        scratch_shapes=[
            pltpu.VMEM((owners - 1, lines, half), jnp.bfloat16),
            pltpu.VMEM((n_dp, lines // 2, down.shape[0]), jnp.float32),
            pltpu.VMEM(down.shape, jnp.bfloat16),
            pltpu.SemaphoreType.DMA,
            dma,
            dma,
        ],
        compiler_params=pltpu.CompilerParams(
            collective_id=2, has_side_effects=True, vmem_limit_bytes=40 << 20
        ),
    )(x, outgoing, down, w)


def slots_of(index, owner_share, owners, capacity):
    streams = index.shape[0]
    owner = index // owner_share
    position = jnp.arange(streams, dtype=jnp.int32)
    before = (owner[:, None] == owner[None, :]) & (position[None, :] < position[:, None])
    slot = owner * capacity + jnp.sum(before.astype(jnp.int32), axis=1)
    return jnp.arange(owners * capacity, dtype=jnp.int32)[:, None] == slot[None, :]


def adapted(x, index, sibling_index, down_factor, up_factor, w, capacity, steps):
    n_dp = lax.axis_size("dp")
    parts = lax.axis_size("tensor")
    owners = n_dp * parts
    streams = index.shape[0]
    owner_share, channels, rank = down_factor.shape
    width = w.shape[1]
    group, mine = lax.axis_index("dp"), lax.axis_index("tensor")
    match = slots_of(index, owner_share, owners, capacity)
    same = jnp.eye(steps, dtype=jnp.bool_)
    spread_out = (
        match.reshape(owners, 1, capacity, 1, streams) & same[None, :, None, :, None]
    ).astype(jnp.bfloat16).reshape(owners, steps * capacity, steps * streams)
    flat = spread_out.reshape(owners * steps * capacity, steps * streams)
    half = x.shape[1] // 2
    sides = [
        jnp.dot(flat, x[:, side * half : (side + 1) * half], preferred_element_type=jnp.float32)
        .astype(jnp.bfloat16)
        .reshape(owners, steps * capacity, half)
        for side in range(2)
    ]
    outgoing = jnp.concatenate(sides, axis=1)
    down = jnp.transpose(down_factor, (0, 2, 1)).reshape(owner_share * rank, channels)
    base, coef = dispatched(x, outgoing, down, w, n_dp, parts)
    me = group * parts + mine
    keeps = []
    for source in range(n_dp):
        held = jnp.where(group == source, index, sibling_index)
        match_in = slots_of(held, owner_share, owners, capacity).reshape(owners, capacity, streams)
        match_in = lax.dynamic_index_in_dim(match_in, me, 0, keepdims=False)
        local = jnp.sum(jnp.where(match_in, (held % owner_share)[None, :], 0), axis=1)
        keep = local[:, None] == jnp.arange(owner_share, dtype=jnp.int32)[None, :]
        keeps.append(jnp.tile(jnp.repeat(keep, rank, axis=1), (steps, 1)))
    coeffs = jnp.where(jnp.stack(keeps), coef, 0.0).astype(jnp.bfloat16)
    delta = jnp.dot(
        coeffs.reshape(n_dp * steps * capacity, owner_share * rank),
        up_factor.reshape(owner_share * rank, width),
        preferred_element_type=jnp.float32,
    ).astype(jnp.bfloat16)
    delta = delta.reshape(n_dp, steps * capacity, width)
    back = lax.all_to_all(delta, "dp", split_axis=0, concat_axis=0, tiled=True)
    spot = lax.dynamic_index_in_dim(
        spread_out.reshape(n_dp, parts, steps * capacity, steps * streams), mine, 1, keepdims=False
    ).reshape(n_dp * steps * capacity, steps * streams).T
    total = scattered(base, spot, back.reshape(n_dp * steps * capacity, width), parts)
    return jnp.transpose(total.reshape(steps, streams, width // parts), (1, 0, 2))


def body(
    convolution_branch_input,
    gate_branch_input,
    convolution_state,
    initial_hidden_state,
    stream_adapter_index,
    convolution_weight,
    convolution_bias,
    input_coefficient_projection,
    step_size_norm_gain,
    step_size_projection,
    step_size_bias,
    negated_diagonal,
    channel_skip_gain,
    output_projection,
    adapter_down_factor,
    adapter_up_factor,
):
    n_dp = lax.axis_size("dp")
    tensor_parts = lax.axis_size("tensor")
    owners = n_dp * tensor_parts
    streams, steps, channel_count = convolution_branch_input.shape
    dt_rank = step_size_norm_gain.shape[0]
    states = negated_diagonal.shape[0]
    kernel = convolution_weight.shape[0]
    width = output_projection.shape[1]
    slice_part = width // tensor_parts
    owner_share = adapter_down_factor.shape[0]
    rank_width = adapter_down_factor.shape[2]
    capacity = max(2, 2 * streams // owners)
    full = jnp.concatenate([convolution_state, convolution_branch_input], axis=1)
    state = initial_hidden_state
    gathered = []
    conv_outs = []
    for step in range(steps):
        window = full[:, step : step + kernel].astype(jnp.float32)
        mixed = jnp.sum(window * convolution_weight[None], axis=1) + convolution_bias
        conv_outs.append(jax.nn.silu(mixed))
    conv_low = jnp.concatenate(conv_outs, axis=0).astype(jnp.bfloat16)
    partial_proj = jnp.dot(
        conv_low, input_coefficient_projection, preferred_element_type=jnp.float32
    )
    small = tensor_parts == 8 and n_dp == 2
    if small:
        dt_all, coef_all = summed_and_normed(
            partial_proj, step_size_norm_gain, tensor_parts, dt_rank
        )
    else:
        projected = lax.psum(partial_proj, "tensor")
        dt_raw = projected[:, :dt_rank]
        factor = lax.rsqrt(jnp.mean(dt_raw * dt_raw, axis=1, keepdims=True) + 1e-06)
        dt_all = (dt_raw * factor * step_size_norm_gain).astype(jnp.bfloat16)
        coef_all = projected[:, dt_rank:]
    for step in range(steps):
        conv_out = conv_outs[step]
        dt_low = dt_all[step * streams : (step + 1) * streams]
        coef = coef_all[step * streams : (step + 1) * streams]
        in_coef = coef[:, :states]
        out_coef = coef[:, states:]
        step_size = jax.nn.softplus(
            jnp.dot(dt_low, step_size_projection, preferred_element_type=jnp.float32)
            + step_size_bias
        )
        decay = jnp.exp(-step_size[:, None, :] * negated_diagonal[None])
        state = decay * state + step_size[:, None, :] * in_coef[:, :, None] * conv_out[:, None, :]
        read = jnp.sum(state * out_coef[:, :, None], axis=1) + channel_skip_gain * conv_out
        gated = read * jax.nn.silu(gate_branch_input[:, step].astype(jnp.float32))
        gathered.append(gated.astype(jnp.bfloat16))
    if small:
        sibling_index = lax.ppermute(stream_adapter_index, "dp", ((0, 1), (1, 0)))
        layer_out = adapted(
            jnp.concatenate(gathered, axis=0),
            stream_adapter_index,
            sibling_index,
            adapter_down_factor,
            adapter_up_factor,
            output_projection,
            capacity,
            steps,
        )
        return (layer_out, state)
    inner_y = jnp.stack(gathered, axis=1)
    owner = stream_adapter_index // owner_share
    local = stream_adapter_index % owner_share
    position = jnp.arange(streams, dtype=jnp.int32)
    before = (owner[:, None] == owner[None, :]) & (position[None, :] < position[:, None])
    current_tally = jnp.sum(before.astype(jnp.int32), axis=1)
    slot = owner * capacity + current_tally
    match = jnp.arange(owners * capacity, dtype=jnp.int32)[:, None] == slot[None, :]
    dispatch = match.astype(jnp.bfloat16)
    slot_local = jnp.sum(jnp.where(match, local[None, :], 0), axis=1).reshape(owners, capacity)
    outgoing = jnp.dot(
        dispatch,
        inner_y.reshape(streams, steps * channel_count),
        preferred_element_type=jnp.float32,
    )
    outgoing = outgoing.astype(jnp.bfloat16).reshape(owners, capacity, steps, channel_count)
    down_factor = adapter_down_factor.reshape(owner_share, tensor_parts, channel_count, rank_width)
    rows = lax.all_to_all(outgoing, ("dp", "tensor"), split_axis=0, concat_axis=0, tiled=True)
    idents = lax.all_to_all(slot_local, ("dp", "tensor"), split_axis=0, concat_axis=0, tiled=True)
    count = rows.shape[1]
    rows = rows.reshape(n_dp, tensor_parts, count, steps, channel_count)
    which = idents.reshape(n_dp, tensor_parts, count)[:, 0]
    select = (which[..., None] == jnp.arange(owner_share, dtype=jnp.int32)).astype(jnp.float32)
    every = jnp.einsum("itksc,atcr->iksar", rows, down_factor, preferred_element_type=jnp.float32)
    coeffs = jnp.einsum("iksar,ika->iksr", every, select).astype(jnp.bfloat16)
    up_factor_split = adapter_up_factor.reshape(owner_share, rank_width, tensor_parts, slice_part)
    spread = jnp.einsum(
        "iksr,arjc->ijksac", coeffs, up_factor_split, preferred_element_type=jnp.float32
    )
    delta = jnp.einsum("ijksac,ika->ijksc", spread, select).astype(jnp.bfloat16)
    delta = delta.reshape(owners, count, steps, slice_part)
    back = lax.all_to_all(delta, ("dp", "tensor"), split_axis=0, concat_axis=0, tiled=True)
    flat_rows = inner_y.reshape(streams * steps, channel_count)
    partial_value = jnp.dot(flat_rows, output_projection, preferred_element_type=jnp.float32)
    total = lax.psum_scatter(
        partial_value.reshape(streams, steps, width), "tensor", scatter_dimension=2, tiled=True
    )
    carried = jnp.dot(
        dispatch.T,
        back.reshape(owners * capacity, steps * slice_part),
        preferred_element_type=jnp.float32,
    )
    layer_out = (total + carried.reshape(streams, steps, slice_part)).astype(jnp.bfloat16)
    return (layer_out, state)


def solution(mesh):
    placed = (
        P(("groups", "dp"), None, "tensor"),
        P(("groups", "dp"), None, "tensor"),
        P(("groups", "dp"), None, "tensor"),
        P(("groups", "dp"), None, "tensor"),
        P(("groups", "dp")),
        P(None, "tensor"),
        P("tensor"),
        P("tensor", None),
        P(),
        P(None, "tensor"),
        P("tensor"),
        P(None, "tensor"),
        P("tensor"),
        P("tensor", None),
        P(("dp", "tensor"), None, None),
        P(("dp", "tensor"), None, None),
    )
    return jax.shard_map(
        body,
        mesh=mesh,
        in_specs=placed,
        out_specs=(P(("groups", "dp"), None, "tensor"), P(("groups", "dp"), None, "tensor")),
        check_vma=False,
    )
```
